32 devices in a mesh: load: 4 (over z), tile: 8 (over y, x, core).
Axes of the slice: x: 2, y: 2, z: 4, core: 2. Of those that a mesh axis runs over, the one named last changes fastest.
Arguments:
- u_prev: float32 [4, 3, 64, 16, 128], P('load', None, 'tile'), may hold values from -0.5 to 0.5
- density: float32 [64, 16, 128], P('tile'), may hold values from 0.3 to 1
- active_blocks: int32 [8, 2, 16], P('tile'), may hold values 0 or 1
- fixed_nodes: int32 [64, 16, 128], P('tile'), may hold values 0 or 1
- load_nodes: int32 [4, 32], P('load'), may hold values from 0 to 131071
- load_forces: float32 [4, 3, 32], P('load'), may hold values from -5 to 5
Outputs:
- displacement: float32 [4, 3, 64, 16, 128], P('load', None, 'tile')
- sensitivity: float32 [64, 16, 128], P('tile')
The draws below stay inside these ranges and needn't reach their ends.
All inputs are finite; a program needn't handle non-finite values. No bound on the sum of `active_blocks` or of `fixed_nodes` on one device may be relied on, other than what follows from the above.
Results may differ from the reference program's by a relative error of at most 0.0003.
Values sent between devices are 32-bit elements; how exact they have to be, the bound alone decides.
A program may use at most 64 MiB of HBM per device.

```python
import math
import jax
import jax.numpy as jnp
import numpy as np
from jax import lax

NY = 16
NZ = 128
NPTS = 32
ITERS = 2
BLOCK = 8
NX = 64
LOADS = 4


def mode_shape(extent, frequency):
    position = (extent - jnp.arange(extent, dtype=jnp.float32)) / extent
    return jnp.sin(0.5 * math.pi * frequency * position)


def draw_u_prev(key, part):
    triples = ((1.0, 3.0, 5.0), (3.0, 5.0, 1.0), (5.0, 1.0, 3.0))
    jitter = jax.random.uniform(jax.random.fold_in(key, 1), (LOADS, 3, NX, NY, NZ), jnp.float32, -1.0, 1.0)
    amplitude = 0.1 * jax.random.normal(jax.random.fold_in(key, 2), (LOADS, 3, 3), jnp.float32)
    smooth_field = jnp.zeros((LOADS, 3, NX, NY, NZ), jnp.float32)
    for index in range(3):
        along_x = mode_shape(NX, triples[index][0])
        along_y = mode_shape(NY, triples[index][1])
        along_z = mode_shape(NZ, triples[index][2])
        product = along_x[:, None, None] * along_y[None, :, None] * along_z[None, None, :]
        smooth_field = smooth_field + amplitude[:, :, index, None, None, None] * product[None, None]
    return jnp.clip(smooth_field + 0.06 * jitter, -0.5, 0.5)


def draw_load_nodes(key, part):
    lower_pick = jax.random.randint(jax.random.fold_in(key, 11), (LOADS, NPTS), 0, NX)
    upper_pick = jax.random.randint(jax.random.fold_in(key, 12), (LOADS, NPTS), 0, NX)
    plane_index = jnp.maximum(lower_pick, upper_pick)
    row_index = jax.random.randint(jax.random.fold_in(key, 13), (LOADS, NPTS), 0, NY)
    depth_index = jax.random.randint(jax.random.fold_in(key, 14), (LOADS, NPTS), 0, NZ)
    return (plane_index * (NY * NZ) + row_index * NZ + depth_index).astype(jnp.int32)


def with_ends(drawn, stream_key, smallest, high):
    shape = drawn.shape
    index_at = [jax.random.randint(jax.random.fold_in(stream_key, axis), (), 0, shape[axis]) for axis in range(len(shape))]
    drawn = drawn.at[tuple(index_at)].set(smallest)
    longest = shape.index(max(shape))
    index_at[longest] = (index_at[longest] + 1) % shape[longest]
    return drawn.at[tuple(index_at)].set(high)


def level_of(own_key, shape, cuts, smallest, high):
    loudness = 1.0
    for axis_at, parts in cuts:
        heights = jax.random.uniform(jax.random.fold_in(jax.random.fold_in(own_key, 6), axis_at), (parts,), jnp.float32, smallest / len(cuts), high / len(cuts))
        loudness = loudness * jnp.repeat(jnp.exp(heights), shape[axis_at] // parts).reshape((-1,) + (1,) * (len(shape) - 1 - axis_at))
    return loudness


def gaussian(rng, shape, deviation, reach, cuts=(), held_as=jnp.bfloat16):
    drawn = deviation * jax.random.normal(rng, shape, jnp.float32)
    if cuts:
        drawn = drawn * level_of(rng, shape, cuts, -0.22, 0.18)
    return jnp.clip(drawn, -reach, reach).astype(held_as)


def setup_inputs(seed: int = 0) -> dict:
    splits = jax.random.split(jax.random.key(seed), 7)
    u_prev = draw_u_prev(jax.random.fold_in(splits[6], 71), 0)
    density = jnp.clip(0.3 + 0.7 * jax.random.uniform(splits[1], (NX, NY, NZ), jnp.float32) ** level_of(splits[1], (NX, NY, NZ), ((0, 8),), -0.2, 0.2), 0.3, 1.0)
    active_blocks = with_ends((jax.random.randint(splits[2], (NX // BLOCK, NY // BLOCK, NZ // BLOCK), 0, 4) < 3).astype(jnp.int32), jax.random.fold_in(splits[2], 1), 0, 1)
    fixed_nodes = with_ends((jax.random.randint(splits[3], (NX, NY, NZ), 0, 16) < 1).astype(jnp.int32), jax.random.fold_in(splits[3], 1), 0, 1)
    load_nodes = draw_load_nodes(jax.random.fold_in(splits[6], 71), 0)
    load_forces = gaussian(splits[5], (LOADS, 3, NPTS), 1.0, 5.0, ((0, 4),), jnp.float32)
    return dict(u_prev=u_prev, density=density, active_blocks=active_blocks, fixed_nodes=fixed_nodes, load_nodes=load_nodes, load_forces=load_forces)


def stiffness_table():
    poisson = 0.3
    lame_first = poisson / ((1.0 + poisson) * (1.0 - 2.0 * poisson))
    shear_modulus = 0.5 / (1.0 + poisson)
    elastic = np.zeros((6, 6))
    elastic[:3, :3] = lame_first
    for component in range(3):
        elastic[component, component] += 2.0 * shear_modulus
        elastic[component + 3, component + 3] = shear_modulus
    gauss_points = [0.5 - 0.5 / math.sqrt(3.0), 0.5 + 0.5 / math.sqrt(3.0)]
    stiffness = np.zeros((24, 24))
    for point_x in gauss_points:
        for point_y in gauss_points:
            for point_z in gauss_points:
                strain = np.zeros((6, 24))
                for corner in range(8):
                    bit_x = corner & 1
                    bit_y = corner >> 1 & 1
                    bit_z = corner >> 2 & 1
                    shape_x = point_x if bit_x == 1 else 1.0 - point_x
                    shape_y = point_y if bit_y == 1 else 1.0 - point_y
                    shape_z = point_z if bit_z == 1 else 1.0 - point_z
                    slope_x = 1.0 if bit_x == 1 else -1.0
                    slope_y = 1.0 if bit_y == 1 else -1.0
                    slope_z = 1.0 if bit_z == 1 else -1.0
                    grad_x = slope_x * shape_y * shape_z
                    grad_y = shape_x * slope_y * shape_z
                    grad_z = shape_x * shape_y * slope_z
                    column = 3 * corner
                    strain[0, column] = grad_x
                    strain[1, column + 1] = grad_y
                    strain[2, column + 2] = grad_z
                    strain[3, column + 1] = grad_z
                    strain[3, column + 2] = grad_y
                    strain[4, column] = grad_z
                    strain[4, column + 2] = grad_x
                    strain[5, column] = grad_y
                    strain[5, column + 1] = grad_x
                stiffness += 0.125 * strain.T @ elastic @ strain
    return stiffness.astype(np.float32)

def corner_bits(corner):
    return (corner & 1, corner >> 1 & 1, corner >> 2 & 1)

def corner_slices(widened):
    planes = widened.shape[1] - 1
    size_y = widened.shape[2]
    size_z = widened.shape[3]
    padded = jnp.pad(widened, ((0, 0), (0, 0), (0, 1), (0, 1)))
    pieces = []
    for corner in range(8):
        bit_x, bit_y, bit_z = corner_bits(corner)
        pieces.append(padded[:, bit_x:bit_x + planes, bit_y:bit_y + size_y, bit_z:bit_z + size_z])
    return pieces

def spread_corner(values, corner):
    bit_x, bit_y, bit_z = corner_bits(corner)
    padded = jnp.pad(values, ((0, 0), (bit_x, 1 - bit_x), (bit_y, 1 - bit_y), (bit_z, 1 - bit_z)))
    return padded[:, :, :-1, :-1]

def corner_force(pieces, stiffness, target):
    summed = jnp.zeros(pieces[0].shape, jnp.float32)
    for source in range(8):
        block_matrix = jnp.asarray(stiffness[3 * target:3 * target + 3, 3 * source:3 * source + 3])
        summed = summed + jnp.tensordot(block_matrix, pieces[source], axes=1, precision=lax.Precision.HIGHEST)
    return summed

def apply_element(widened, weight):
    pieces = corner_slices(widened)
    stiffness = stiffness_table()
    summed = None
    for target in range(8):
        term = spread_corner(corner_force(pieces, stiffness, target) * weight[None], target)
        summed = term if summed is None else summed + term
    return summed

def diagonal_sum(weight):
    stiffness = stiffness_table()
    summed = None
    for target in range(8):
        entries = [float(stiffness[3 * target + c, 3 * target + c]) for c in range(3)]
        column = jnp.asarray(entries, dtype=jnp.float32).reshape(3, 1, 1, 1)
        term = spread_corner(column * weight[None], target)
        summed = term if summed is None else summed + term
    return summed

def element_energy(widened):
    pieces = corner_slices(widened)
    stiffness = stiffness_table()
    energy = None
    for target in range(8):
        term = lax.optimization_barrier(jnp.sum(pieces[target] * corner_force(pieces, stiffness, target), axis=0))
        energy = term if energy is None else energy + term
    return energy

def expand_blocks(blocks):
    grown = jnp.repeat(jnp.repeat(jnp.repeat(blocks, BLOCK, 0), BLOCK, 1), BLOCK, 2)
    return (grown == 1).astype(jnp.float32)

def reference(u_prev, density, active_blocks, fixed_nodes, load_nodes, load_forces):
    active = expand_blocks(active_blocks)
    weight = density * density * density * active
    upper_pad = ((0, 0), (0, 1), (0, 0), (0, 0))
    diagonal = diagonal_sum(weight)[:, :NX]
    free_mask = ((fixed_nodes[None] == 0) & (diagonal > 0.0)).astype(jnp.float32)
    inverse = free_mask / (diagonal + 1.0 - free_mask)

    def operate(vector):
        return free_mask * apply_element(jnp.pad(vector, upper_pad), weight)[:, :NX]

    def solve_case(inputs):
        initial, node_ids, forces = inputs
        force_field = jnp.zeros((3, NX * NY * NZ), jnp.float32).at[:, node_ids].add(forces)
        force_field = force_field.reshape(3, NX, NY, NZ)
        solution = free_mask * initial
        residual = free_mask * force_field - operate(solution)
        precond = inverse * residual
        direction = precond
        inner_now = jnp.sum(residual * precond)
        for iteration in range(ITERS):
            applied = operate(direction)
            step_size = inner_now / jnp.sum(direction * applied)
            solution = solution + step_size * direction
            residual = residual - step_size * applied
            if iteration + 1 < ITERS:
                precond = inverse * residual
                inner_next = jnp.sum(residual * precond)
                direction = precond + inner_next / inner_now * direction
                inner_now = inner_next
        energy = element_energy(jnp.pad(solution, upper_pad))
        return (solution, energy)
    displacement, energies = lax.map(solve_case, (u_prev, load_nodes, load_forces))
    sensitivity = -3.0 / LOADS * density * density * active * lax.optimization_barrier(jnp.sum(energies, axis=0))
    return (displacement, sensitivity)
```

```python
import functools

import jax
import jax.numpy as jnp
from jax import lax
from jax.experimental import pallas as pl
from jax.experimental.pallas import tpu as pltpu
from jax.sharding import PartitionSpec as P

BLOCK = 8
DEEP = 3
CHUNK = 1
POISSON = 0.3
LAM = POISSON / ((1.0 + POISSON) * (1.0 - 2.0 * POISSON))
MU = 0.5 / (1.0 + POISSON)
DIAG = (LAM + 4.0 * MU) / 9.0
MESH = pl.DeviceIdType.MESH


def up(array, axis):
    size = array.shape[axis]
    spot = lax.broadcasted_iota(jnp.int32, array.shape, axis)
    return jnp.where(spot == size - 1, 0.0, pltpu.roll(array, size - 1, axis))


def down(array, axis):
    spot = lax.broadcasted_iota(jnp.int32, array.shape, axis)
    return jnp.where(spot == 0, 0.0, pltpu.roll(array, 1, axis))


def flat_modes(plane):
    above = up(plane, 2)
    modes = {}
    for key, part in (("S", plane + above), ("D", above - plane)):
        beyond = up(part, 1)
        modes["S" + key] = part + beyond
        modes["D" + key] = beyond - part
    return modes


def cube_modes(low, high):
    modes = []
    for first, second in zip(low, high):
        own = {}
        for key in first:
            if key != "SS":
                own["S" + key] = first[key] + second[key]
            own["D" + key] = second[key] - first[key]
        modes.append(own)
    return modes


def mode_forces(modes, weight):
    u, v, w = modes
    first, middle, last = weight * (1.0 / 16.0), weight * (1.0 / 48.0), weight * ((LAM + 4.0 * MU) / 144.0)
    fu, fv, fw = {}, {}, {}
    trace = LAM * (u["DSS"] + v["SDS"] + w["SSD"])
    fu["DSS"] = first * (trace + 2.0 * MU * u["DSS"])
    fv["SDS"] = first * (trace + 2.0 * MU * v["SDS"])
    fw["SSD"] = first * (trace + 2.0 * MU * w["SSD"])
    for one, other, fone, fother, ka, kb in (
        (u, w, fu, fw, "DDS", "SDD"),
        (v, w, fv, fw, "DDS", "DSD"),
        (u, v, fu, fv, "DSD", "SDD"),
    ):
        trace = LAM * (one[ka] + other[kb])
        fone[ka] = middle * (trace + 3.0 * MU * one[ka])
        fother[kb] = middle * (trace + 3.0 * MU * other[kb])
    fu["DDD"] = last * u["DDD"]
    fv["DDD"] = last * v["DDD"]
    fw["DDD"] = last * w["DDD"]
    shear = first * MU
    fu["SDS"] = fv["DSS"] = shear * (u["SDS"] + v["DSS"])
    fu["SSD"] = fw["DSS"] = shear * (u["SSD"] + w["DSS"])
    fv["SSD"] = fw["SDS"] = shear * (v["SSD"] + w["SDS"])
    bend = middle * MU
    total = u["SDD"] + v["DSD"] + w["DDS"]
    fu["SDD"] = bend * (total + u["SDD"])
    fv["DSD"] = bend * (total + v["DSD"])
    fw["DDS"] = bend * (total + w["DDS"])
    return fu, fv, fw


def mode_energy(modes):
    u, v, w = modes

    def sq(x):
        return x * x

    first = LAM * sq(u["DSS"] + v["SDS"] + w["SSD"]) + 2.0 * MU * (sq(u["DSS"]) + sq(v["SDS"]) + sq(w["SSD"]))
    first = first + MU * (sq(u["SDS"] + v["DSS"]) + sq(u["SSD"] + w["DSS"]) + sq(v["SSD"] + w["SDS"]))
    pairs = ((u["DDS"], w["SDD"]), (v["DDS"], w["DSD"]), (u["DSD"], v["SDD"]))
    traces = sum(sq(a + b) for a, b in pairs)
    squares = sum(sq(a) + sq(b) for a, b in pairs)
    a, b, c = u["SDD"], v["DSD"], w["DDS"]
    middle = LAM * traces + 3.0 * MU * squares + MU * (sq(a + b) + sq(a + c) + sq(b + c))
    last = (LAM + 4.0 * MU) * (sq(u["DDD"]) + sq(v["DDD"]) + sq(w["DDD"]))
    return first * (1.0 / 16.0) + middle * (1.0 / 48.0) + last * (1.0 / 144.0)


def spread(modes):
    along = {}
    for key in "SD":
        total, delta = modes["S" + key], modes["D" + key]
        along[key] = (total - delta) + down(total + delta, 1)
    return (along["S"] - along["D"]) + down(along["S"] + along["D"], 2)


def stiffness(planes_of, weight_of, store, count):
    low = [flat_modes(field) for field in planes_of(0)]
    carry = None
    for element in range(count):
        high = [flat_modes(field) for field in planes_of(element + 1)]
        forces = mode_forces(cube_modes(low, high), weight_of(element))
        lower, upper = [], []
        for force in forces:
            lower.append({k: force["S" + k] - force["D" + k] if k != "SS" else -force["D" + k] for k in ("SS", "SD", "DS", "DD")})
            upper.append({k: force["S" + k] + force["D" + k] if k != "SS" else force["D" + k] for k in ("SS", "SD", "DS", "DD")})
        if carry is not None:
            store(element, [spread({k: a[k] + b[k] for k in a}) for a, b in zip(carry, lower)])
        carry = upper
        low = high


def fold(array):
    return jnp.sum(jnp.sum(array, axis=0), axis=0, keepdims=True)


def kernel(tiles, loads, u_ref, density_ref, blocks_ref, fixed_ref, nodes_ref, forces_ref,
           out_ref, sens_ref,
           ext, inv_s, free_s, force_s, r_s, z_s, q_s, w_s, aw_s, red, red2, en, parts, final,
           halo_send, halo_recv, red_send, red_recv, red2_send, red2_recv,
           part_send, part_recv, final_send, final_recv):
    me = lax.axis_index("tile")
    mine = lax.axis_index("load")
    planes, ny, nz = density_ref.shape
    tile_peers = [lax.rem(me + k, tiles) for k in range(1, tiles)]
    load_peers = [lax.rem(mine + k, loads) for k in range(1, loads)]

    barrier = pltpu.get_barrier_semaphore()
    for peer in tile_peers:
        pl.semaphore_signal(barrier, inc=1, device_id=(mine, peer), device_id_type=MESH)
    for peer in load_peers:
        pl.semaphore_signal(barrier, inc=1, device_id=(peer, me), device_id_type=MESH)

    widen = (lax.broadcasted_iota(jnp.int32, (nz // BLOCK, nz), 1) // BLOCK
             == lax.broadcasted_iota(jnp.int32, (nz // BLOCK, nz), 0)).astype(jnp.float32)
    rows = lax.broadcasted_iota(jnp.int32, (ny, nz // BLOCK), 0) // BLOCK
    masks = []
    for bx in range(planes // BLOCK):
        tall = jnp.zeros((ny, nz // BLOCK), jnp.float32)
        for by in range(ny // BLOCK):
            marked = (blocks_ref[bx, by:by + 1, :] == 1).astype(jnp.float32)
            tall = jnp.where(rows == by, marked, tall)
        masks.append(jnp.dot(tall, widen, preferred_element_type=jnp.float32))
    for plane in range(planes):
        dens = density_ref[plane]
        held = (fixed_ref[plane] != 0).astype(jnp.float32)
        ext[3, DEEP + plane] = dens * dens * dens * masks[plane // BLOCK]
        ext[4, DEEP + plane] = held
        for c in range(3):
            ext[c, DEEP + plane] = u_ref[0, c, plane] * (1.0 - held)

    pl.semaphore_wait(barrier, tiles + loads - 2)

    def halo(way):
        if way == 0:
            return pltpu.make_async_remote_copy(
                src_ref=ext.at[:, DEEP:2 * DEEP], dst_ref=ext.at[:, planes + DEEP:planes + 2 * DEEP],
                send_sem=halo_send.at[0], recv_sem=halo_recv.at[0],
                device_id=(mine, jnp.maximum(me - 1, 0)), device_id_type=MESH)
        return pltpu.make_async_remote_copy(
            src_ref=ext.at[:, planes:planes + DEEP], dst_ref=ext.at[:, 0:DEEP],
            send_sem=halo_send.at[1], recv_sem=halo_recv.at[1],
            device_id=(mine, jnp.minimum(me + 1, tiles - 1)), device_id_type=MESH)

    @pl.when(me > 0)
    def _():
        halo(0).start()

    @pl.when(me < tiles - 1)
    def _():
        halo(1).start()

    wide = planes + 4
    base = (me * planes - 2) * ny
    ids = nodes_ref[...]
    row_of = ids // nz - base
    lane_of = lax.rem(ids, nz)
    points = ids.shape[1]
    pick_row = (lax.broadcasted_iota(jnp.int32, (wide * ny, points), 0) == row_of).astype(jnp.float32)
    pick_lane = (lax.broadcasted_iota(jnp.int32, (nz, points), 0) == lane_of).astype(jnp.float32)
    for c in range(3):
        placed = pick_lane * forces_ref[0, c:c + 1, :]
        force_s[c] = lax.dot_general(pick_row, placed, (((1,), (1,)), ((), ())),
                                     precision=lax.Precision.HIGHEST,
                                     preferred_element_type=jnp.float32).reshape(wide, ny, nz)

    @pl.when(me == 0)
    def _():
        ext[:, 0:DEEP] = jnp.zeros((5, DEEP, ny, nz), jnp.float32)

    @pl.when(me == tiles - 1)
    def _():
        ext[0:4, planes + DEEP:planes + 2 * DEEP] = jnp.zeros((4, DEEP, ny, nz), jnp.float32)
        ext[4:5, planes + DEEP:planes + 2 * DEEP] = jnp.ones((1, DEEP, ny, nz), jnp.float32)

    @pl.when(me < tiles - 1)
    def _():
        halo(0).wait_recv()

    @pl.when(me > 0)
    def _():
        halo(1).wait_recv()

    def summed(plane):
        weight = ext[3, plane:plane + 1]
        part = weight + down(weight, 2)
        return part + down(part, 1)

    before = summed(0)
    for node in range(wide):
        after = summed(node + 1)
        diagonal = DIAG * (before + after)
        free = jnp.where((ext[4, node + 1:node + 2] == 0.0) & (diagonal > 0.0), 1.0, 0.0)
        free_s[node:node + 1] = free
        inv_s[node:node + 1] = free / (diagonal + 1.0 - free)
        before = after

    def store_residual(node, image):
        at = node - 1
        free, inv = free_s[at:at + 1], inv_s[at:at + 1]
        for c in range(3):
            left = free * (force_s[c, at:at + 1] - image[c])
            r_s[c, at:at + 1] = left
            z_s[c, at:at + 1] = inv * left

    stiffness(lambda i: [ext[c, i:i + 1] for c in range(3)],
              lambda e: ext[3, e:e + 1], store_residual, planes + 5)

    def store_image(node, image):
        at = node - 1
        free, inv = free_s[node:node + 1], inv_s[node:node + 1]
        for c in range(3):
            q = free * image[c]
            q_s[c, at:at + 1] = q
            w_s[c, at:at + 1] = inv * q

    stiffness(lambda i: [z_s[c, i:i + 1] for c in range(3)],
              lambda e: ext[3, e + 1:e + 2], store_image, planes + 3)

    def gather(slots, send, recv, values):
        row = lax.broadcasted_iota(jnp.int32, (8, nz), 0)
        block = jnp.zeros((8, nz), jnp.float32)
        for index, value in enumerate(values):
            block = jnp.where(row == index, value, block)
        slots[me] = block
        copies = []
        for k, peer in enumerate(tile_peers):
            copy = pltpu.make_async_remote_copy(
                src_ref=slots.at[me], dst_ref=slots.at[me],
                send_sem=send.at[k], recv_sem=recv.at[k],
                device_id=(mine, peer), device_id_type=MESH)
            copy.start()
            copies.append(copy)
        return copies

    def total(slots, copies):
        for copy in copies:
            copy.wait_recv()
        block = slots[0]
        for t in range(1, tiles):
            block = block + slots[t]
        return jnp.sum(block, axis=1, keepdims=True)

    def dot(pairs):
        return fold(sum(a * b for a, b in pairs))

    own = [(r_s[c, 2:2 + planes], z_s[c, 2:2 + planes], q_s[c, 1:1 + planes]) for c in range(3)]
    copies1 = gather(red, red_send, red_recv,
                     [dot([(r, z) for r, z, q in own]), dot([(z, q) for r, z, q in own])])

    def store_second(node, image):
        at = node - 1
        free = free_s[node + 1:node + 2]
        for c in range(3):
            aw_s[c, at:at + 1] = free * image[c]

    stiffness(lambda i: [w_s[c, i:i + 1] for c in range(3)],
              lambda e: ext[3, e + 2:e + 3], store_second, planes + 1)

    sums = total(red, copies1)
    inner, curve = sums[0:1, :], sums[1:2, :]
    alpha = inner / curve
    g_parts, s_parts, t_parts = [], [], []
    for c in range(3):
        q = q_s[c, 1:1 + planes]
        r1 = r_s[c, 2:2 + planes] - alpha[None] * q
        z1 = z_s[c, 2:2 + planes] - alpha[None] * w_s[c, 1:1 + planes]
        g_parts.append((r1, z1))
        s_parts.append((z1, q - alpha[None] * aw_s[c]))
        t_parts.append((z1, q))
    copies2 = gather(red2, red2_send, red2_recv, [dot(g_parts), dot(s_parts), dot(t_parts)])
    sums = total(red2, copies2)
    inner2, second, cross = sums[0:1, :], sums[1:2, :], sums[2:3, :]
    beta = inner2 / inner
    alpha2 = inner2 / (second + 2.0 * beta * cross + beta * beta * curve)
    by_z = (alpha + alpha2 * (1.0 + beta))[None]
    by_w = (alpha2 * alpha)[None]

    low = None
    for plane in range(planes + 1):
        fields = []
        free = free_s[plane + 2:plane + 3]
        for c in range(3):
            moved = free * ext[c, DEEP + plane:DEEP + plane + 1]
            moved = moved + by_z * z_s[c, plane + 2:plane + 3] - by_w * w_s[c, plane + 1:plane + 2]
            if plane < planes:
                out_ref[0, c, plane:plane + 1] = moved
            fields.append(moved)
        high = [flat_modes(field) for field in fields]
        if plane > 0:
            en[(plane - 1) * ny:plane * ny, :] = mode_energy(cube_modes(low, high))[0]
        low = high

    share = planes * ny // loads
    copies3 = []
    for k, peer in enumerate(load_peers):
        copy = pltpu.make_async_remote_copy(
            src_ref=en.at[pl.ds(pl.multiple_of(peer * share, 8), share)], dst_ref=parts.at[k],
            send_sem=part_send.at[k], recv_sem=part_recv.at[k],
            device_id=(peer, me), device_id_type=MESH)
        copy.start()
        copies3.append(copy)
    here = pl.ds(pl.multiple_of(mine * share, 8), share)
    energy = en[here]
    for k, copy in enumerate(copies3):
        copy.wait_recv()
        energy = energy + parts[k]
    final[here] = energy
    copies4 = []
    for k, peer in enumerate(load_peers):
        copy = pltpu.make_async_remote_copy(
            src_ref=final.at[here], dst_ref=final.at[here],
            send_sem=final_send.at[k], recv_sem=final_recv.at[k],
            device_id=(peer, me), device_id_type=MESH)
        copy.start()
        copies4.append(copy)
    for copy in copies4:
        copy.wait_recv()
    for plane in range(planes):
        dens = density_ref[plane]
        sens_ref[plane] = (-3.0 / loads) * dens * dens * masks[plane // BLOCK] * final[plane * ny:(plane + 1) * ny, :]

    @pl.when(me > 0)
    def _():
        halo(0).wait_send()

    @pl.when(me < tiles - 1)
    def _():
        halo(1).wait_send()

    for copy in copies1 + copies2 + copies3 + copies4:
        copy.wait_send()


def shards(tiles, loads, u_prev, density, active_blocks, fixed_nodes, load_nodes, load_forces):
    planes, ny, nz = density.shape
    wide = planes + 4
    vmem = pl.BlockSpec(memory_space=pltpu.VMEM)
    dma = pltpu.SemaphoreType.DMA

    def field(count, *lead):
        return pltpu.VMEM((*lead, count, ny, nz), jnp.float32)

    share = planes * ny // loads
    return pl.pallas_call(
        functools.partial(kernel, tiles, loads),
        out_shape=(jax.ShapeDtypeStruct(u_prev.shape, jnp.float32),
                   jax.ShapeDtypeStruct(density.shape, jnp.float32)),
        in_specs=[vmem] * 6,
        out_specs=(vmem, vmem),
        scratch_shapes=[
            field(planes + 2 * DEEP, 5),
            field(wide), field(wide), field(wide, 3),
            field(wide, 3), field(wide, 3), field(planes + 2, 3), field(planes + 2, 3), field(planes, 3),
            pltpu.VMEM((tiles, 8, nz), jnp.float32), pltpu.VMEM((tiles, 8, nz), jnp.float32),
            pltpu.VMEM((planes * ny, nz), jnp.float32),
            pltpu.VMEM((loads - 1, share, nz), jnp.float32),
            pltpu.VMEM((planes * ny, nz), jnp.float32),
            dma((2,)), dma((2,)),
            dma((tiles - 1,)), dma((tiles - 1,)), dma((tiles - 1,)), dma((tiles - 1,)),
            dma((loads - 1,)), dma((loads - 1,)), dma((loads - 1,)), dma((loads - 1,)),
        ],
        compiler_params=pltpu.CompilerParams(
            collective_id=0, has_side_effects=True, vmem_limit_bytes=32 * 1024 * 1024),
    )(u_prev, density, active_blocks, fixed_nodes, load_nodes, load_forces)


def solution(mesh):
    in_specs = (
        P("load", None, "tile", None, None),
        P("tile", None, None),
        P("tile", None, None),
        P("tile", None, None),
        P("load", None),
        P("load", None, None),
    )
    out_specs = (P("load", None, "tile", None, None), P("tile", None, None))
    body = functools.partial(shards, mesh.shape["tile"], mesh.shape["load"])
    return jax.shard_map(body, mesh=mesh, in_specs=in_specs, out_specs=out_specs, check_vma=False)
```

```python
import functools

import jax
import jax.numpy as jnp
from jax import lax
from jax.experimental import pallas as pl
from jax.experimental.pallas import tpu as pltpu
from jax.sharding import PartitionSpec as P

BLOCK = 8
DEEP = 3
CHUNK = 1
POISSON = 0.3
LAM = POISSON / ((1.0 + POISSON) * (1.0 - 2.0 * POISSON))
MU = 0.5 / (1.0 + POISSON)
DIAG = (LAM + 4.0 * MU) / 9.0
MESH = pl.DeviceIdType.MESH


def up(array, axis):
    size = array.shape[axis]
    spot = lax.broadcasted_iota(jnp.int32, array.shape, axis)
    return jnp.where(spot == size - 1, 0.0, pltpu.roll(array, size - 1, axis))


def down(array, axis):
    spot = lax.broadcasted_iota(jnp.int32, array.shape, axis)
    return jnp.where(spot == 0, 0.0, pltpu.roll(array, 1, axis))


def flat_modes(plane):
    above = up(plane, 2)
    modes = {}
    for key, part in (("S", plane + above), ("D", above - plane)):
        beyond = up(part, 1)
        modes["S" + key] = part + beyond
        modes["D" + key] = beyond - part
    return modes


def cube_modes(low, high):
    modes = []
    for first, second in zip(low, high):
        own = {}
        for key in first:
            if key != "SS":
                own["S" + key] = first[key] + second[key]
            own["D" + key] = second[key] - first[key]
        modes.append(own)
    return modes


def mode_forces(modes, weight):
    u, v, w = modes
    first, middle, last = weight * (1.0 / 16.0), weight * (1.0 / 48.0), weight * ((LAM + 4.0 * MU) / 144.0)
    fu, fv, fw = {}, {}, {}
    trace = LAM * (u["DSS"] + v["SDS"] + w["SSD"])
    fu["DSS"] = first * (trace + 2.0 * MU * u["DSS"])
    fv["SDS"] = first * (trace + 2.0 * MU * v["SDS"])
    fw["SSD"] = first * (trace + 2.0 * MU * w["SSD"])
    for one, other, fone, fother, ka, kb in (
        (u, w, fu, fw, "DDS", "SDD"),
        (v, w, fv, fw, "DDS", "DSD"),
        (u, v, fu, fv, "DSD", "SDD"),
    ):
        trace = LAM * (one[ka] + other[kb])
        fone[ka] = middle * (trace + 3.0 * MU * one[ka])
        fother[kb] = middle * (trace + 3.0 * MU * other[kb])
    fu["DDD"] = last * u["DDD"]
    fv["DDD"] = last * v["DDD"]
    fw["DDD"] = last * w["DDD"]
    shear = first * MU
    fu["SDS"] = fv["DSS"] = shear * (u["SDS"] + v["DSS"])
    fu["SSD"] = fw["DSS"] = shear * (u["SSD"] + w["DSS"])
    fv["SSD"] = fw["SDS"] = shear * (v["SSD"] + w["SDS"])
    bend = middle * MU
    total = u["SDD"] + v["DSD"] + w["DDS"]
    fu["SDD"] = bend * (total + u["SDD"])
    fv["DSD"] = bend * (total + v["DSD"])
    fw["DDS"] = bend * (total + w["DDS"])
    return fu, fv, fw


def mode_energy(modes):
    u, v, w = modes

    def sq(x):
        return x * x

    first = LAM * sq(u["DSS"] + v["SDS"] + w["SSD"]) + 2.0 * MU * (sq(u["DSS"]) + sq(v["SDS"]) + sq(w["SSD"]))
    first = first + MU * (sq(u["SDS"] + v["DSS"]) + sq(u["SSD"] + w["DSS"]) + sq(v["SSD"] + w["SDS"]))
    pairs = ((u["DDS"], w["SDD"]), (v["DDS"], w["DSD"]), (u["DSD"], v["SDD"]))
    traces = sum(sq(a + b) for a, b in pairs)
    squares = sum(sq(a) + sq(b) for a, b in pairs)
    a, b, c = u["SDD"], v["DSD"], w["DDS"]
    middle = LAM * traces + 3.0 * MU * squares + MU * (sq(a + b) + sq(a + c) + sq(b + c))
    last = (LAM + 4.0 * MU) * (sq(u["DDD"]) + sq(v["DDD"]) + sq(w["DDD"]))
    return first * (1.0 / 16.0) + middle * (1.0 / 48.0) + last * (1.0 / 144.0)


def spread(modes):
    along = {}
    for key in "SD":
        total, delta = modes["S" + key], modes["D" + key]
        along[key] = (total - delta) + down(total + delta, 1)
    return (along["S"] - along["D"]) + down(along["S"] + along["D"], 2)


def stiffness(planes_of, weight_of, store, count):
    low = [flat_modes(field) for field in planes_of(0)]
    carry = None
    for element in range(count):
        high = [flat_modes(field) for field in planes_of(element + 1)]
        forces = mode_forces(cube_modes(low, high), weight_of(element))
        lower, upper = [], []
        for force in forces:
            lower.append({k: force["S" + k] - force["D" + k] if k != "SS" else -force["D" + k] for k in ("SS", "SD", "DS", "DD")})
            upper.append({k: force["S" + k] + force["D" + k] if k != "SS" else force["D" + k] for k in ("SS", "SD", "DS", "DD")})
        if carry is not None:
            store(element, [spread({k: a[k] + b[k] for k in a}) for a, b in zip(carry, lower)])
        carry = upper
        low = high


def fold(array):
    return jnp.sum(jnp.sum(array, axis=0), axis=0, keepdims=True)


def kernel(tiles, loads, u_in, density_in, blocks_in, fixed_in, nodes_in, forces_in,
           out_hbm, sens_ref,
           out_ref, out_sem,
           u_ref, density_ref, blocks_ref, fixed_ref, nodes_ref, forces_ref, in_sem, ext, inv_s, free_s, force_s, r_s, z_s, q_s, w_s, aw_s, move_s, red, en, parts, final,
           halo_send, halo_recv, red_send, red_recv,
           part_send, part_recv, final_send, final_recv):
    me = lax.axis_index("tile")
    mine = lax.axis_index("load")
    planes, ny, nz = density_ref.shape
    tile_peers = [lax.rem(me + k, tiles) for k in range(1, tiles)]
    load_peers = [lax.rem(mine + k, loads) for k in range(1, loads)]

    arrivals = []
    for index, (source, target) in enumerate((
            (density_in, density_ref), (fixed_in, fixed_ref), (blocks_in, blocks_ref),
            (u_in, u_ref), (nodes_in, nodes_ref), (forces_in, forces_ref))):
        arrival = pltpu.make_async_copy(source, target, in_sem.at[index])
        arrival.start()
        arrivals.append(arrival)
    barrier = pltpu.get_barrier_semaphore()
    for peer in tile_peers:
        pl.semaphore_signal(barrier, inc=1, device_id=(mine, peer), device_id_type=MESH)
    for peer in load_peers:
        pl.semaphore_signal(barrier, inc=1, device_id=(peer, me), device_id_type=MESH)

    widen = (lax.broadcasted_iota(jnp.int32, (nz // BLOCK, nz), 1) // BLOCK
             == lax.broadcasted_iota(jnp.int32, (nz // BLOCK, nz), 0)).astype(jnp.float32)
    rows = lax.broadcasted_iota(jnp.int32, (ny, nz // BLOCK), 0) // BLOCK
    for arrival in arrivals:
        arrival.wait()
    masks = []
    for bx in range(planes // BLOCK):
        tall = jnp.zeros((ny, nz // BLOCK), jnp.float32)
        for by in range(ny // BLOCK):
            marked = (blocks_ref[bx, by:by + 1, :] == 1).astype(jnp.float32)
            tall = jnp.where(rows == by, marked, tall)
        masks.append(jnp.dot(tall, widen, preferred_element_type=jnp.float32))
    for plane in range(planes):
        dens = density_ref[plane]
        held = (fixed_ref[plane] != 0).astype(jnp.float32)
        ext[3, DEEP + plane] = dens * dens * dens * masks[plane // BLOCK]
        ext[4, DEEP + plane] = held
        for c in range(3):
            ext[c, DEEP + plane] = u_ref[0, c, plane] * (1.0 - held)

    pl.semaphore_wait(barrier, tiles + loads - 2)

    def halo(way):
        if way == 0:
            return pltpu.make_async_remote_copy(
                src_ref=ext.at[:, DEEP:2 * DEEP], dst_ref=ext.at[:, planes + DEEP:planes + 2 * DEEP],
                send_sem=halo_send.at[0], recv_sem=halo_recv.at[0],
                device_id=(mine, jnp.maximum(me - 1, 0)), device_id_type=MESH)
        return pltpu.make_async_remote_copy(
            src_ref=ext.at[:, planes:planes + DEEP], dst_ref=ext.at[:, 0:DEEP],
            send_sem=halo_send.at[1], recv_sem=halo_recv.at[1],
            device_id=(mine, jnp.minimum(me + 1, tiles - 1)), device_id_type=MESH)

    @pl.when(me > 0)
    def _():
        halo(0).start()

    @pl.when(me < tiles - 1)
    def _():
        halo(1).start()

    wide = planes + 4
    base = (me * planes - 2) * ny
    ids = nodes_ref[...]
    row_of = ids // nz - base
    lane_of = lax.rem(ids, nz)
    points = ids.shape[1]
    pick_row = (lax.broadcasted_iota(jnp.int32, (wide * ny, points), 0) == row_of).astype(jnp.float32)
    pick_lane = (lax.broadcasted_iota(jnp.int32, (nz, points), 0) == lane_of).astype(jnp.float32)
    for c in range(3):
        placed = pick_lane * forces_ref[c]
        force_s[c] = lax.dot_general(pick_row, placed, (((1,), (1,)), ((), ())),
                                     precision=lax.Precision.HIGHEST,
                                     preferred_element_type=jnp.float32).reshape(wide, ny, nz)

    @pl.when(me == 0)
    def _():
        ext[:, 0:DEEP] = jnp.zeros((5, DEEP, ny, nz), jnp.float32)

    @pl.when(me == tiles - 1)
    def _():
        ext[0:4, planes + DEEP:planes + 2 * DEEP] = jnp.zeros((4, DEEP, ny, nz), jnp.float32)
        ext[4:5, planes + DEEP:planes + 2 * DEEP] = jnp.ones((1, DEEP, ny, nz), jnp.float32)

    @pl.when(me < tiles - 1)
    def _():
        halo(0).wait_recv()

    @pl.when(me > 0)
    def _():
        halo(1).wait_recv()

    def summed(plane):
        weight = ext[3, plane:plane + 1]
        part = weight + down(weight, 2)
        return part + down(part, 1)

    before = summed(0)
    for node in range(wide):
        after = summed(node + 1)
        diagonal = DIAG * (before + after)
        free = jnp.where((ext[4, node + 1:node + 2] == 0.0) & (diagonal > 0.0), 1.0, 0.0)
        free_s[node:node + 1] = free
        inv_s[node:node + 1] = free / (diagonal + 1.0 - free)
        before = after

    def store_residual(node, image):
        at = node - 1
        free, inv = free_s[at:at + 1], inv_s[at:at + 1]
        for c in range(3):
            left = free * (force_s[c, at:at + 1] - image[c])
            r_s[c, at:at + 1] = left
            z_s[c, at:at + 1] = inv * left

    stiffness(lambda i: [ext[c, i:i + 1] for c in range(3)],
              lambda e: ext[3, e:e + 1], store_residual, planes + 5)

    def store_image(node, image):
        at = node - 1
        free, inv = free_s[node:node + 1], inv_s[node:node + 1]
        for c in range(3):
            q = free * image[c]
            q_s[c, at:at + 1] = q
            w_s[c, at:at + 1] = inv * q

    stiffness(lambda i: [z_s[c, i:i + 1] for c in range(3)],
              lambda e: ext[3, e + 1:e + 2], store_image, planes + 3)

    def gather(slots, send, recv, values):
        row = lax.broadcasted_iota(jnp.int32, (8, nz), 0)
        block = jnp.zeros((8, nz), jnp.float32)
        for index, value in enumerate(values):
            block = jnp.where(row == index, value, block)
        slots[me] = block
        copies = []
        for k, peer in enumerate(tile_peers):
            copy = pltpu.make_async_remote_copy(
                src_ref=slots.at[me], dst_ref=slots.at[me],
                send_sem=send.at[k], recv_sem=recv.at[k],
                device_id=(mine, peer), device_id_type=MESH)
            copy.start()
            copies.append(copy)
        return copies

    def total(slots, copies):
        for copy in copies:
            copy.wait_recv()
        block = slots[0]
        for t in range(1, tiles):
            block = block + slots[t]
        return jnp.sum(block, axis=1, keepdims=True)

    def dot(pairs):
        return fold(sum(a * b for a, b in pairs))

    own = [(r_s[c, 2:2 + planes], z_s[c, 2:2 + planes], q_s[c, 1:1 + planes]) for c in range(3)]
    def store_second(node, image):
        at = node - 1
        free = free_s[node + 1:node + 2]
        for c in range(3):
            aw_s[c, at:at + 1] = free * image[c]

    stiffness(lambda i: [w_s[c, i:i + 1] for c in range(3)],
              lambda e: ext[3, e + 2:e + 3], store_second, planes + 1)

    seconds = [(w_s[c, 1:1 + planes], q_s[c, 1:1 + planes], aw_s[c]) for c in range(3)]
    copies1 = gather(red, red_send, red_recv,
                     [dot([(r, z) for r, z, q in own]), dot([(z, q) for r, z, q in own]),
                      dot([(w, q) for w, q, image in seconds]), dot([(w, image) for w, q, image in seconds])])
    sums = total(red, copies1)
    inner, curve, square, bent = sums[0:1, :], sums[1:2, :], sums[2:3, :], sums[3:4, :]
    alpha = inner / curve
    inner2 = inner - 2.0 * alpha * curve + alpha * alpha * square
    beta = inner2 / inner
    cross = curve - alpha * square
    second = curve - 2.0 * alpha * square + alpha * alpha * bent
    alpha2 = inner2 / (second + 2.0 * beta * cross + beta * beta * curve)
    by_z = (alpha + alpha2 * (1.0 + beta))[None]
    by_w = (alpha2 * alpha)[None]

    for plane in range(planes + 1):
        free = free_s[plane + 2:plane + 3]
        for c in range(3):
            moved = free * ext[c, DEEP + plane:DEEP + plane + 1]
            moved = moved + by_z * z_s[c, plane + 2:plane + 3] - by_w * w_s[c, plane + 1:plane + 2]
            if plane < planes:
                out_ref[0, c, plane:plane + 1] = moved
            move_s[c, plane:plane + 1] = moved

    leaving = pltpu.make_async_copy(out_ref, out_hbm, out_sem)
    leaving.start()

    def energies(start, count):
        low = None
        for step in range(count + 1):
            high = [flat_modes(move_s[c, pl.ds(start + step, 1)]) for c in range(3)]
            if step > 0:
                spot = (start + step - 1) * ny
                if not isinstance(spot, int):
                    spot = pl.multiple_of(spot, 8)
                en[pl.ds(spot, ny), :] = mode_energy(cube_modes(low, high))[0]
            low = high

    share = planes * ny // loads
    by_share = share % ny == 0
    if not by_share:
        energies(0, planes)
    copies3 = []
    for k, peer in enumerate(load_peers):
        if by_share:
            energies(peer * (share // ny), share // ny)
        copy = pltpu.make_async_remote_copy(
            src_ref=en.at[pl.ds(pl.multiple_of(peer * share, 8), share)], dst_ref=parts.at[k],
            send_sem=part_send.at[k], recv_sem=part_recv.at[k],
            device_id=(peer, me), device_id_type=MESH)
        copy.start()
        copies3.append(copy)
    if by_share:
        energies(mine * (share // ny), share // ny)
    here = pl.ds(pl.multiple_of(mine * share, 8), share)
    energy = en[here]
    for k, copy in enumerate(copies3):
        copy.wait_recv()
        energy = energy + parts[k]
    final[here] = energy
    copies4 = []
    for k, peer in enumerate(load_peers):
        copy = pltpu.make_async_remote_copy(
            src_ref=final.at[here], dst_ref=final.at[here],
            send_sem=final_send.at[k], recv_sem=final_recv.at[k],
            device_id=(peer, me), device_id_type=MESH)
        copy.start()
        copies4.append(copy)
    for copy in copies4:
        copy.wait_recv()
    for plane in range(planes):
        dens = density_ref[plane]
        sens_ref[plane] = (-3.0 / loads) * dens * dens * masks[plane // BLOCK] * final[plane * ny:(plane + 1) * ny, :]

    @pl.when(me > 0)
    def _():
        halo(0).wait_send()

    @pl.when(me < tiles - 1)
    def _():
        halo(1).wait_send()

    leaving.wait()
    for copy in copies1 + copies3 + copies4:
        copy.wait_send()


def shards(tiles, loads, u_prev, density, active_blocks, fixed_nodes, load_nodes, load_forces):
    planes, ny, nz = density.shape
    wide = planes + 4
    vmem = pl.BlockSpec(memory_space=pltpu.VMEM)
    dma = pltpu.SemaphoreType.DMA

    def field(count, *lead):
        return pltpu.VMEM((*lead, count, ny, nz), jnp.float32)

    share = planes * ny // loads
    return pl.pallas_call(
        functools.partial(kernel, tiles, loads),
        out_shape=(jax.ShapeDtypeStruct(u_prev.shape, jnp.float32),
                   jax.ShapeDtypeStruct(density.shape, jnp.float32)),
        in_specs=[pl.BlockSpec(memory_space=pltpu.HBM)] * 6,
        out_specs=(pl.BlockSpec(memory_space=pltpu.HBM), vmem),
        scratch_shapes=[
            pltpu.VMEM(u_prev.shape, jnp.float32), dma(()),
            pltpu.VMEM(u_prev.shape, jnp.float32), pltpu.VMEM(density.shape, jnp.float32),
            pltpu.VMEM(active_blocks.shape, jnp.int32), pltpu.VMEM(fixed_nodes.shape, jnp.int32),
            pltpu.VMEM(load_nodes.shape, jnp.int32), pltpu.VMEM((3, 1, load_forces.shape[2]), jnp.float32),
            dma((6,)),
            field(planes + 2 * DEEP, 5),
            field(wide), field(wide), field(wide, 3),
            field(wide, 3), field(wide, 3), field(planes + 2, 3), field(planes + 2, 3), field(planes, 3), field(planes + 1, 3),
            pltpu.VMEM((tiles, 8, nz), jnp.float32),
            pltpu.VMEM((planes * ny, nz), jnp.float32),
            pltpu.VMEM((loads - 1, share, nz), jnp.float32),
            pltpu.VMEM((planes * ny, nz), jnp.float32),
            dma((2,)), dma((2,)),
            dma((tiles - 1,)), dma((tiles - 1,)),
            dma((loads - 1,)), dma((loads - 1,)), dma((loads - 1,)), dma((loads - 1,)),
        ],
        compiler_params=pltpu.CompilerParams(
            collective_id=0, has_side_effects=True, vmem_limit_bytes=58 * 1024 * 1024),
    )(u_prev, density, active_blocks, fixed_nodes, load_nodes, load_forces.transpose(1, 0, 2))


def solution(mesh):
    in_specs = (
        P("load", None, "tile", None, None),
        P("tile", None, None),
        P("tile", None, None),
        P("tile", None, None),
        P("load", None),
        P("load", None, None),
    )
    out_specs = (P("load", None, "tile", None, None), P("tile", None, None))
    body = functools.partial(shards, mesh.shape["tile"], mesh.shape["load"])
    return jax.shard_map(body, mesh=mesh, in_specs=in_specs, out_specs=out_specs, check_vma=False)
```

```python
import functools

import jax
import jax.numpy as jnp
from jax import lax
from jax.experimental import pallas as pl
from jax.experimental.pallas import tpu as pltpu
from jax.sharding import PartitionSpec as P

BLOCK = 8
DEEP = 3
CHUNK = 1
POISSON = 0.3
LAM = POISSON / ((1.0 + POISSON) * (1.0 - 2.0 * POISSON))
MU = 0.5 / (1.0 + POISSON)
DIAG = (LAM + 4.0 * MU) / 9.0
MESH = pl.DeviceIdType.MESH


def up(array, axis):
    size = array.shape[axis]
    spot = lax.broadcasted_iota(jnp.int32, array.shape, axis)
    return jnp.where(spot == size - 1, 0.0, pltpu.roll(array, size - 1, axis))


def down(array, axis):
    spot = lax.broadcasted_iota(jnp.int32, array.shape, axis)
    return jnp.where(spot == 0, 0.0, pltpu.roll(array, 1, axis))


def flat_modes(plane):
    above = up(plane, 2)
    modes = {}
    for key, part in (("S", plane + above), ("D", above - plane)):
        beyond = up(part, 1)
        modes["S" + key] = part + beyond
        modes["D" + key] = beyond - part
    return modes


def cube_modes(low, high):
    modes = []
    for first, second in zip(low, high):
        own = {}
        for key in first:
            if key != "SS":
                own["S" + key] = first[key] + second[key]
            own["D" + key] = second[key] - first[key]
        modes.append(own)
    return modes


def mode_forces(modes, weight):
    u, v, w = modes
    first, middle, last = weight * (1.0 / 16.0), weight * (1.0 / 48.0), weight * ((LAM + 4.0 * MU) / 144.0)
    fu, fv, fw = {}, {}, {}
    trace = LAM * (u["DSS"] + v["SDS"] + w["SSD"])
    fu["DSS"] = first * (trace + 2.0 * MU * u["DSS"])
    fv["SDS"] = first * (trace + 2.0 * MU * v["SDS"])
    fw["SSD"] = first * (trace + 2.0 * MU * w["SSD"])
    for one, other, fone, fother, ka, kb in (
        (u, w, fu, fw, "DDS", "SDD"),
        (v, w, fv, fw, "DDS", "DSD"),
        (u, v, fu, fv, "DSD", "SDD"),
    ):
        trace = LAM * (one[ka] + other[kb])
        fone[ka] = middle * (trace + 3.0 * MU * one[ka])
        fother[kb] = middle * (trace + 3.0 * MU * other[kb])
    fu["DDD"] = last * u["DDD"]
    fv["DDD"] = last * v["DDD"]
    fw["DDD"] = last * w["DDD"]
    shear = first * MU
    fu["SDS"] = fv["DSS"] = shear * (u["SDS"] + v["DSS"])
    fu["SSD"] = fw["DSS"] = shear * (u["SSD"] + w["DSS"])
    fv["SSD"] = fw["SDS"] = shear * (v["SSD"] + w["SDS"])
    bend = middle * MU
    total = u["SDD"] + v["DSD"] + w["DDS"]
    fu["SDD"] = bend * (total + u["SDD"])
    fv["DSD"] = bend * (total + v["DSD"])
    fw["DDS"] = bend * (total + w["DDS"])
    return fu, fv, fw


def mode_energy(modes):
    u, v, w = modes

    def sq(x):
        return x * x

    first = LAM * sq(u["DSS"] + v["SDS"] + w["SSD"]) + 2.0 * MU * (sq(u["DSS"]) + sq(v["SDS"]) + sq(w["SSD"]))
    first = first + MU * (sq(u["SDS"] + v["DSS"]) + sq(u["SSD"] + w["DSS"]) + sq(v["SSD"] + w["SDS"]))
    pairs = ((u["DDS"], w["SDD"]), (v["DDS"], w["DSD"]), (u["DSD"], v["SDD"]))
    traces = sum(sq(a + b) for a, b in pairs)
    squares = sum(sq(a) + sq(b) for a, b in pairs)
    a, b, c = u["SDD"], v["DSD"], w["DDS"]
    middle = LAM * traces + 3.0 * MU * squares + MU * (sq(a + b) + sq(a + c) + sq(b + c))
    last = (LAM + 4.0 * MU) * (sq(u["DDD"]) + sq(v["DDD"]) + sq(w["DDD"]))
    return first * (1.0 / 16.0) + middle * (1.0 / 48.0) + last * (1.0 / 144.0)


def spread(modes):
    along = {}
    for key in "SD":
        total, delta = modes["S" + key], modes["D" + key]
        along[key] = (total - delta) + down(total + delta, 1)
    return (along["S"] - along["D"]) + down(along["S"] + along["D"], 2)


def stiffness(planes_of, weight_of, store, count):
    low = [flat_modes(field) for field in planes_of(0)]
    carry = None
    for element in range(count):
        high = [flat_modes(field) for field in planes_of(element + 1)]
        forces = mode_forces(cube_modes(low, high), weight_of(element))
        lower, upper = [], []
        for force in forces:
            lower.append({k: force["S" + k] - force["D" + k] if k != "SS" else -force["D" + k] for k in ("SS", "SD", "DS", "DD")})
            upper.append({k: force["S" + k] + force["D" + k] if k != "SS" else force["D" + k] for k in ("SS", "SD", "DS", "DD")})
        if carry is not None:
            store(element, [spread({k: a[k] + b[k] for k in a}) for a, b in zip(carry, lower)])
        carry = upper
        low = high


def fold(array):
    return jnp.sum(jnp.sum(array, axis=0), axis=0, keepdims=True)


def kernel(tiles, loads, u_in, density_in, blocks_in, fixed_in, nodes_in, forces_in,
           out_ref, sens_ref,
           u_ref, density_ref, blocks_ref, fixed_ref, nodes_ref, forces_ref, in_sem, ext, inv_s, free_s, force_s, r_s, z_s, q_s, w_s, aw_s, move_s, red, en, parts, final,
           halo_send, halo_recv, red_send, red_recv,
           part_send, part_recv, final_send, final_recv):
    me = lax.axis_index("tile")
    mine = lax.axis_index("load")
    planes, ny, nz = density_ref.shape
    tile_peers = [lax.rem(me + k, tiles) for k in range(1, tiles)]
    load_peers = [lax.rem(mine + k, loads) for k in range(1, loads)]

    arrivals = []
    for index, (source, target) in enumerate((
            (density_in, density_ref), (fixed_in, fixed_ref), (blocks_in, blocks_ref),
            (u_in, u_ref), (nodes_in, nodes_ref), (forces_in, forces_ref))):
        arrival = pltpu.make_async_copy(source, target, in_sem.at[index])
        arrival.start()
        arrivals.append(arrival)
    barrier = pltpu.get_barrier_semaphore()
    for peer in tile_peers:
        pl.semaphore_signal(barrier, inc=1, device_id=(mine, peer), device_id_type=MESH)
    for peer in load_peers:
        pl.semaphore_signal(barrier, inc=1, device_id=(peer, me), device_id_type=MESH)

    widen = (lax.broadcasted_iota(jnp.int32, (nz // BLOCK, nz), 1) // BLOCK
             == lax.broadcasted_iota(jnp.int32, (nz // BLOCK, nz), 0)).astype(jnp.float32)
    rows = lax.broadcasted_iota(jnp.int32, (ny, nz // BLOCK), 0) // BLOCK
    for arrival in arrivals:
        arrival.wait()
    masks = []
    for bx in range(planes // BLOCK):
        tall = jnp.zeros((ny, nz // BLOCK), jnp.float32)
        for by in range(ny // BLOCK):
            marked = (blocks_ref[bx, by:by + 1, :] == 1).astype(jnp.float32)
            tall = jnp.where(rows == by, marked, tall)
        masks.append(jnp.dot(tall, widen, preferred_element_type=jnp.float32))
    for plane in range(planes):
        dens = density_ref[plane]
        held = (fixed_ref[plane] != 0).astype(jnp.float32)
        ext[3, DEEP + plane] = dens * dens * dens * masks[plane // BLOCK]
        ext[4, DEEP + plane] = held
        for c in range(3):
            ext[c, DEEP + plane] = u_ref[0, c, plane] * (1.0 - held)

    pl.semaphore_wait(barrier, tiles + loads - 2)

    def halo(way):
        if way == 0:
            return pltpu.make_async_remote_copy(
                src_ref=ext.at[:, DEEP:2 * DEEP], dst_ref=ext.at[:, planes + DEEP:planes + 2 * DEEP],
                send_sem=halo_send.at[0], recv_sem=halo_recv.at[0],
                device_id=(mine, jnp.maximum(me - 1, 0)), device_id_type=MESH)
        return pltpu.make_async_remote_copy(
            src_ref=ext.at[:, planes:planes + DEEP], dst_ref=ext.at[:, 0:DEEP],
            send_sem=halo_send.at[1], recv_sem=halo_recv.at[1],
            device_id=(mine, jnp.minimum(me + 1, tiles - 1)), device_id_type=MESH)

    @pl.when(me > 0)
    def _():
        halo(0).start()

    @pl.when(me < tiles - 1)
    def _():
        halo(1).start()

    wide = planes + 4
    base = (me * planes - 2) * ny
    ids = nodes_ref[...]
    row_of = ids // nz - base
    lane_of = lax.rem(ids, nz)
    points = ids.shape[1]
    pick_row = (lax.broadcasted_iota(jnp.int32, (wide * ny, points), 0) == row_of).astype(jnp.float32)
    pick_lane = (lax.broadcasted_iota(jnp.int32, (nz, points), 0) == lane_of).astype(jnp.float32)
    for c in range(3):
        placed = pick_lane * forces_ref[c]
        force_s[c] = lax.dot_general(pick_row, placed, (((1,), (1,)), ((), ())),
                                     precision=lax.Precision.HIGHEST,
                                     preferred_element_type=jnp.float32).reshape(wide, ny, nz)

    def summed(plane):
        weight = ext[3, plane:plane + 1]
        part = weight + down(weight, 2)
        return part + down(part, 1)

    def masks_of(first, last):
        before = summed(first)
        for node in range(first, last):
            after = summed(node + 1)
            diagonal = DIAG * (before + after)
            free = jnp.where((ext[4, node + 1:node + 2] == 0.0) & (diagonal > 0.0), 1.0, 0.0)
            free_s[node:node + 1] = free
            inv_s[node:node + 1] = free / (diagonal + 1.0 - free)
            before = after

    def residual(first, last):
        masks_of(first, last)

        def store_residual(node, image):
            at = node + first - 1
            free, inv = free_s[at:at + 1], inv_s[at:at + 1]
            for c in range(3):
                left = free * (force_s[c, at:at + 1] - image[c])
                r_s[c, at:at + 1] = left
                z_s[c, at:at + 1] = inv * left

        stiffness(lambda i: [ext[c, first + i:first + i + 1] for c in range(3)],
                  lambda e: ext[3, first + e:first + e + 1], store_residual, last - first + 1)

    residual(3, planes + 1)

    @pl.when(me == 0)
    def _():
        ext[:, 0:DEEP] = jnp.zeros((5, DEEP, ny, nz), jnp.float32)

    @pl.when(me == tiles - 1)
    def _():
        ext[0:4, planes + DEEP:planes + 2 * DEEP] = jnp.zeros((4, DEEP, ny, nz), jnp.float32)
        ext[4:5, planes + DEEP:planes + 2 * DEEP] = jnp.ones((1, DEEP, ny, nz), jnp.float32)

    @pl.when(me < tiles - 1)
    def _():
        halo(0).wait_recv()

    @pl.when(me > 0)
    def _():
        halo(1).wait_recv()

    residual(0, 3)
    residual(planes + 1, wide)

    def store_image(node, image):
        at = node - 1
        free, inv = free_s[node:node + 1], inv_s[node:node + 1]
        for c in range(3):
            q = free * image[c]
            q_s[c, at:at + 1] = q
            w_s[c, at:at + 1] = inv * q

    stiffness(lambda i: [z_s[c, i:i + 1] for c in range(3)],
              lambda e: ext[3, e + 1:e + 2], store_image, planes + 3)

    def gather(slots, send, recv, values):
        row = lax.broadcasted_iota(jnp.int32, (8, nz), 0)
        block = jnp.zeros((8, nz), jnp.float32)
        for index, value in enumerate(values):
            block = jnp.where(row == index, value, block)
        slots[me] = block
        copies = []
        for k, peer in enumerate(tile_peers):
            copy = pltpu.make_async_remote_copy(
                src_ref=slots.at[me], dst_ref=slots.at[me],
                send_sem=send.at[k], recv_sem=recv.at[k],
                device_id=(mine, peer), device_id_type=MESH)
            copy.start()
            copies.append(copy)
        return copies

    def total(slots, copies):
        for copy in copies:
            copy.wait_recv()
        block = slots[0]
        for t in range(1, tiles):
            block = block + slots[t]
        return jnp.sum(block, axis=1, keepdims=True)

    def dot(pairs):
        return fold(sum(a * b for a, b in pairs))

    own = [(r_s[c, 2:2 + planes], z_s[c, 2:2 + planes], q_s[c, 1:1 + planes]) for c in range(3)]
    def store_second(node, image):
        at = node - 1
        free = free_s[node + 1:node + 2]
        for c in range(3):
            aw_s[c, at:at + 1] = free * image[c]

    stiffness(lambda i: [w_s[c, i:i + 1] for c in range(3)],
              lambda e: ext[3, e + 2:e + 3], store_second, planes + 1)

    seconds = [(w_s[c, 1:1 + planes], q_s[c, 1:1 + planes], aw_s[c]) for c in range(3)]
    copies1 = gather(red, red_send, red_recv,
                     [dot([(r, z) for r, z, q in own]), dot([(z, q) for r, z, q in own]),
                      dot([(w, q) for w, q, image in seconds]), dot([(w, image) for w, q, image in seconds])])
    sums = total(red, copies1)
    inner, curve, square, bent = sums[0:1, :], sums[1:2, :], sums[2:3, :], sums[3:4, :]
    alpha = inner / curve
    inner2 = inner - 2.0 * alpha * curve + alpha * alpha * square
    beta = inner2 / inner
    cross = curve - alpha * square
    second = curve - 2.0 * alpha * square + alpha * alpha * bent
    alpha2 = inner2 / (second + 2.0 * beta * cross + beta * beta * curve)
    by_z = (alpha + alpha2 * (1.0 + beta))[None]
    by_w = (alpha2 * alpha)[None]

    for plane in range(planes + 1):
        free = free_s[plane + 2:plane + 3]
        for c in range(3):
            moved = free * ext[c, DEEP + plane:DEEP + plane + 1]
            moved = moved + by_z * z_s[c, plane + 2:plane + 3] - by_w * w_s[c, plane + 1:plane + 2]
            if plane < planes:
                out_ref[0, c, plane:plane + 1] = moved
            move_s[c, plane:plane + 1] = moved

    def energies(start, count):
        low = None
        for step in range(count + 1):
            high = [flat_modes(move_s[c, pl.ds(start + step, 1)]) for c in range(3)]
            if step > 0:
                spot = (start + step - 1) * ny
                if not isinstance(spot, int):
                    spot = pl.multiple_of(spot, 8)
                en[pl.ds(spot, ny), :] = mode_energy(cube_modes(low, high))[0]
            low = high

    share = planes * ny // loads
    by_share = share % ny == 0
    if not by_share:
        energies(0, planes)
    copies3 = []
    for k, peer in enumerate(load_peers):
        if by_share:
            energies(peer * (share // ny), share // ny)
        copy = pltpu.make_async_remote_copy(
            src_ref=en.at[pl.ds(pl.multiple_of(peer * share, 8), share)], dst_ref=parts.at[k],
            send_sem=part_send.at[k], recv_sem=part_recv.at[k],
            device_id=(peer, me), device_id_type=MESH)
        copy.start()
        copies3.append(copy)
    if by_share:
        energies(mine * (share // ny), share // ny)
    here = pl.ds(pl.multiple_of(mine * share, 8), share)
    energy = en[here]
    for k, copy in enumerate(copies3):
        copy.wait_recv()
        energy = energy + parts[k]
    final[here] = energy
    copies4 = []
    for k, peer in enumerate(load_peers):
        copy = pltpu.make_async_remote_copy(
            src_ref=final.at[here], dst_ref=final.at[here],
            send_sem=final_send.at[k], recv_sem=final_recv.at[k],
            device_id=(peer, me), device_id_type=MESH)
        copy.start()
        copies4.append(copy)
    for copy in copies4:
        copy.wait_recv()
    for plane in range(planes):
        dens = density_ref[plane]
        sens_ref[plane] = (-3.0 / loads) * dens * dens * masks[plane // BLOCK] * final[plane * ny:(plane + 1) * ny, :]

    @pl.when(me > 0)
    def _():
        halo(0).wait_send()

    @pl.when(me < tiles - 1)
    def _():
        halo(1).wait_send()

    for copy in copies1 + copies3 + copies4:
        copy.wait_send()


def shards(tiles, loads, u_prev, density, active_blocks, fixed_nodes, load_nodes, load_forces):
    planes, ny, nz = density.shape
    wide = planes + 4
    vmem = pl.BlockSpec(memory_space=pltpu.VMEM)
    dma = pltpu.SemaphoreType.DMA

    def field(count, *lead):
        return pltpu.VMEM((*lead, count, ny, nz), jnp.float32)

    share = planes * ny // loads
    return pl.pallas_call(
        functools.partial(kernel, tiles, loads),
        out_shape=(jax.ShapeDtypeStruct(u_prev.shape, jnp.float32),
                   jax.ShapeDtypeStruct(density.shape, jnp.float32)),
        in_specs=[pl.BlockSpec(memory_space=pltpu.HBM)] * 6,
        out_specs=(vmem, vmem),
        scratch_shapes=[
            pltpu.VMEM(u_prev.shape, jnp.float32), pltpu.VMEM(density.shape, jnp.float32),
            pltpu.VMEM(active_blocks.shape, jnp.int32), pltpu.VMEM(fixed_nodes.shape, jnp.int32),
            pltpu.VMEM(load_nodes.shape, jnp.int32), pltpu.VMEM((3, 1, load_forces.shape[2]), jnp.float32),
            dma((6,)),
            field(planes + 2 * DEEP, 5),
            field(wide), field(wide), field(wide, 3),
            field(wide, 3), field(wide, 3), field(planes + 2, 3), field(planes + 2, 3), field(planes, 3), field(planes + 1, 3),
            pltpu.VMEM((tiles, 8, nz), jnp.float32),
            pltpu.VMEM((planes * ny, nz), jnp.float32),
            pltpu.VMEM((loads - 1, share, nz), jnp.float32),
            pltpu.VMEM((planes * ny, nz), jnp.float32),
            dma((2,)), dma((2,)),
            dma((tiles - 1,)), dma((tiles - 1,)),
            dma((loads - 1,)), dma((loads - 1,)), dma((loads - 1,)), dma((loads - 1,)),
        ],
        compiler_params=pltpu.CompilerParams(
            collective_id=0, has_side_effects=True, vmem_limit_bytes=32 * 1024 * 1024),
    )(*(pltpu.with_memory_space_constraint(array, pltpu.HBM) for array in (
        u_prev, density, active_blocks, fixed_nodes, load_nodes, load_forces.transpose(1, 0, 2))))


def solution(mesh):
    in_specs = (
        P("load", None, "tile", None, None),
        P("tile", None, None),
        P("tile", None, None),
        P("tile", None, None),
        P("load", None),
        P("load", None, None),
    )
    out_specs = (P("load", None, "tile", None, None), P("tile", None, None))
    body = functools.partial(shards, mesh.shape["tile"], mesh.shape["load"])
    return jax.shard_map(body, mesh=mesh, in_specs=in_specs, out_specs=out_specs, check_vma=False)
```
